256 devices in a mesh: outer: 16 (over z, core), inner: 16 (over y, x).
Axes of the slice: x: 4, y: 4, z: 8, core: 2. Of those that a mesh axis runs over, the one named last changes fastest.
Arguments:
- queries: bfloat16 [2, 64, 8192], P(None, 'outer', 'inner'), may hold values from -7.5 to 7.5
- key_cache: bfloat16 [524288, 1024], P(('outer', 'inner')), may hold values from -8 to 8
- value_cache: bfloat16 [524288, 1024], P(('outer', 'inner')), may hold values from -6 to 6
- new_keys: bfloat16 [2, 64, 1024], P(None, 'outer'), may hold values from -12 to 12
- new_values: bfloat16 [2, 64, 1024], P(None, 'outer'), may hold values from -6 to 6
- lengths: int32 [64], replicated, may hold values from 32768 to 524288, as said below
Outputs:
- attended: bfloat16 [2, 64, 8192], P(None, 'outer', 'inner')
The draws below stay inside these ranges and needn't reach their ends.
Inputs may be any that keep to these rules, and one draw needn't show every extreme that they name: `lengths`: some row uses the whole prefix and some row exactly 32768 positions.
All inputs are finite; a program needn't handle non-finite values.
Results may differ from the reference program's by a relative error of at most 0.0024.
Values may be sent and summed in bfloat16 or wider, within the bound.
A program may use at most 128 MiB of HBM per device.

```python
import math
import jax
import jax.numpy as jnp
from jax import lax

HQ = 64
KVH = 8
HD = 128
GROUP = 8
KBLOCK = 256
STEPS = 2
PREFIX = 524288
ROWS = 64


def base_queries(key):
    values = 1.5 * jax.random.normal(jax.random.fold_in(key, 11), (STEPS, ROWS, HQ * HD), jnp.float32)
    return jnp.clip(values, -7.5, 7.5)


def draw_queries(key, part):
    values = base_queries(key)
    return values.astype(jnp.bfloat16)


def draw_key_cache(key, part):
    key = jax.random.fold_in(key, 5)
    cache = jnp.clip(2.0 * jax.random.normal(key, (PREFIX, KVH * HD), jnp.float32), -8.0, 8.0)
    return cache.astype(jnp.bfloat16)


def draw_new_keys(key, part):
    values = base_queries(key)
    key = jax.random.fold_in(key, 7)
    grouped = jnp.mean(values.reshape(STEPS, ROWS, KVH, GROUP, HD), axis=3)
    noise = 0.5 * jax.random.normal(key, (STEPS, ROWS, KVH, HD), jnp.float32)
    result = jnp.clip(5.0 * grouped + noise, -12.0, 12.0)
    return result.reshape(STEPS, ROWS, KVH * HD).astype(jnp.bfloat16)


def draw_lengths(key, part):
    key = jax.random.fold_in(key, 9)
    drawn = jax.random.randint(key, (ROWS,), PREFIX // 16, PREFIX + 1)
    return drawn.at[0].set(PREFIX).at[1].set(PREFIX // 16).astype(jnp.int32)


def steps_of(own_key, shape, shards, least, largest):
    loudness = 1.0
    for dim, blocks in shards:
        draws = jax.random.uniform(jax.random.fold_in(jax.random.fold_in(own_key, 6), dim), (blocks,), jnp.float32, least / len(shards), largest / len(shards))
        loudness = loudness * jnp.repeat(jnp.exp(draws), shape[dim] // blocks).reshape((-1,) + (1,) * (len(shape) - 1 - dim))
    return loudness


def normal_values(rng, dims, deviation, most, pieces=(), held_as=jnp.bfloat16):
    values = deviation * jax.random.normal(rng, dims, jnp.float32)
    if pieces:
        values = values * steps_of(rng, dims, pieces, -0.22, 0.18)
    return jnp.clip(values, -most, most).astype(held_as)


def setup_inputs(seed: int = 0) -> dict:
    splits = jax.random.split(jax.random.key(seed), 7)
    queries = draw_queries(jax.random.fold_in(splits[6], 71), 0)
    key_cache = draw_key_cache(jax.random.fold_in(splits[6], 71), 0)
    value_cache = normal_values(splits[2], (PREFIX, KVH * HD), 1.0, 6.0, ((0, 256),))
    new_keys = draw_new_keys(jax.random.fold_in(splits[6], 71), 0)
    new_values = normal_values(splits[4], (STEPS, ROWS, KVH * HD), 1.0, 6.0, ((1, 16),))
    lengths = draw_lengths(jax.random.fold_in(splits[6], 71), 0)
    return {"queries": queries, "key_cache": key_cache, "value_cache": value_cache, "new_keys": new_keys, "new_values": new_values, "lengths": lengths}


FLOOR = -1e+30

def block_terms(grouped, key_block, value_block, first_position, lengths):
    extent = key_block.shape[0]
    key_float = key_block.reshape(extent, KVH, HD).astype(jnp.float32)
    value_float = value_block.reshape(extent, KVH, HD).astype(jnp.float32)
    scores = jnp.einsum('rkgd,tkd->rkgt', grouped.astype(jnp.float32), key_float) / math.sqrt(HD)
    positions = first_position + jnp.arange(extent, dtype=jnp.int32)
    usable = (positions[None, :] < lengths[:, None])[:, None, None, :]
    highest = lax.optimization_barrier(jnp.max(jnp.where(usable, scores, FLOOR), axis=-1, keepdims=True))
    shifted = jnp.where(usable, scores, highest) - highest
    weights = jnp.where(usable, jnp.exp(shifted), 0.0).astype(jnp.bfloat16)
    totals = lax.optimization_barrier(jnp.sum(weights.astype(jnp.float32), axis=-1, keepdims=True))
    outputs = jnp.einsum('rkgt,tkd->rkgd', weights.astype(jnp.float32), value_float)
    return (highest, totals, outputs)

def combine(first_part, second_part):
    peak_score = jnp.maximum(first_part[0], second_part[0])
    left_factor = jnp.exp(first_part[0] - peak_score)
    right_factor = jnp.exp(second_part[0] - peak_score)
    return (peak_score, left_factor * first_part[1] + right_factor * second_part[1], left_factor * first_part[2] + right_factor * second_part[2])

def finish(highest, totals, outputs, query_float, own_keys, own_values):
    own_scores = [lax.optimization_barrier(jnp.sum(query_float * earlier, axis=-1, keepdims=True)) / math.sqrt(HD) for earlier in own_keys]
    peak_score = highest
    for candidate in own_scores:
        peak_score = jnp.maximum(peak_score, candidate)
    factor = jnp.exp(highest - peak_score)
    numerator = factor * outputs
    denominator = factor * totals
    for candidate, value_row in zip(own_scores, own_values):
        weight_own = jnp.exp(candidate - peak_score)
        numerator = numerator + weight_own * value_row
        denominator = denominator + weight_own
    return (numerator / denominator).reshape(numerator.shape[0], -1).astype(jnp.bfloat16)

def reference(queries, key_cache, value_cache, new_keys, new_values, lengths):
    block_count = key_cache.shape[0] // KBLOCK
    key_blocks = key_cache.reshape(block_count, KBLOCK, KVH * HD)
    value_blocks = value_cache.reshape(block_count, KBLOCK, KVH * HD)
    firsts = jnp.arange(block_count, dtype=jnp.int32) * KBLOCK
    all_rows = queries.shape[1]
    results = []
    for step_index in range(STEPS):
        grouped = queries[step_index].reshape(all_rows, KVH, GROUP, HD)

        def visit(running, block_item):
            return (combine(running, block_terms(grouped, block_item[0], block_item[1], block_item[2], lengths)), None)
        initial = (jnp.full((all_rows, KVH, GROUP, 1), FLOOR, jnp.float32), jnp.zeros((all_rows, KVH, GROUP, 1), jnp.float32), jnp.zeros((all_rows, KVH, GROUP, HD), jnp.float32))
        state, _ = lax.scan(visit, initial, (key_blocks, value_blocks, firsts))
        highest = state[0].reshape(all_rows, HQ, 1)
        totals = state[1].reshape(all_rows, HQ, 1)
        outputs = state[2].reshape(all_rows, HQ, HD)
        query_float = queries[step_index].reshape(all_rows, HQ, HD).astype(jnp.float32)
        own_keys = [jnp.repeat(new_keys[earlier].reshape(all_rows, KVH, HD), GROUP, axis=1).astype(jnp.float32) for earlier in range(step_index + 1)]
        own_values = [jnp.repeat(new_values[earlier].reshape(all_rows, KVH, HD), GROUP, axis=1).astype(jnp.float32) for earlier in range(step_index + 1)]
        results.append(finish(highest, totals, outputs, query_float, own_keys, own_values))
    return jnp.stack(results)
```

```python
import functools
import math

import jax
import jax.numpy as jnp
from jax import lax
from jax.experimental import pallas as pl
from jax.experimental.pallas import tpu as pltpu
from jax.sharding import PartitionSpec as P

HD = 128
GROUP = 8
STEPS = 2
SCALE2 = math.log2(math.e) / math.sqrt(HD)
MASKED = -1e30
LOWEST = -3e38
MESH = pl.DeviceIdType.MESH


def remote(src, dst, send_sem, recv_sem, device):
    return pltpu.make_async_remote_copy(
        src_ref=src, dst_ref=dst, send_sem=send_sem, recv_sem=recv_sem, device_id=device, device_id_type=MESH
    )


def kernel(
    sizes,
    q_ref,
    nk_hbm,
    nv_hbm,
    len_hbm,
    k_hbm,
    v_hbm,
    out_ref,
    nk_ref,
    nv_ref,
    len_ref,
    limits,
    stage,
    qbuf,
    kbuf,
    vbuf,
    qx,
    ax,
    mrun,
    mnext,
    sbuf,
    vt,
    outbuf,
    rbuf,
    zsend,
    zrecv,
    scal,
    small_sem,
    local_sem,
    kv_send,
    kv_recv,
    s1_send,
    s1_recv,
    s2_send,
    s2_recv,
    r_send,
    r_recv,
    z_send,
    z_recv,
):
    NO, NI, KL, EXT, TT, CH, QB, ROWS = sizes
    NZ = NO // 2
    QD = NZ * QB
    NQ = 4 * QD
    LT = min(128, QD)
    ZT = LT // QB
    o = lax.axis_index("outer")
    i = lax.axis_index("inner")
    z, c = o // 2, o % 2
    half_plane = NI // 2
    c_d, j_d, half_d = i // half_plane, (i % half_plane) // 2, i % 2
    mate = (z * 2 + (1 - c), i)

    def cols(head):
        return pl.ds(pl.multiple_of(head * HD, HD), HD)

    def own_kv(j, which):
        src, dst = ((k_hbm, kbuf), (v_hbm, vbuf))[which]
        return pltpu.make_async_copy(src.at[:, cols(c * KL + j)], dst.at[j, c], local_sem.at[j, which])

    def mate_kv(j, which):
        src, dst = ((k_hbm, kbuf), (v_hbm, vbuf))[which]
        return remote(
            src.at[:, cols((1 - c) * KL + j)], dst.at[j, c], kv_send.at[j, which], kv_recv.at[j, which], mate
        )

    def slot_head(k):
        return lax.rem(k + i, KL)

    def each(n, body):
        lax.fori_loop(0, n, lambda s, carry: (body(s), carry)[1], 0)

    small = [
        pltpu.make_async_copy(src, dst, small_sem.at[n])
        for n, (src, dst) in enumerate(((len_hbm, len_ref), (nk_hbm, nk_ref), (nv_hbm, nv_ref)))
    ]
    for copy in small:
        copy.start()

    @functools.partial(each, KL)
    def _(k):
        own_kv(slot_head(k), 0).start()
        own_kv(slot_head(k), 1).start()

    barrier = pltpu.get_barrier_semaphore()

    @functools.partial(each, 2 * NI - 1)
    def _(s):
        other = lax.rem(c * NI + i + s + 1, 2 * NI)
        pl.semaphore_signal(barrier, inc=1, device_id=(z * 2 + other // NI, other % NI), device_id_type=MESH)

    @functools.partial(each, NZ - 1)
    def _(s):
        pl.semaphore_signal(
            barrier, inc=1, device_id=(lax.rem(z + s + 1, NZ) * 2 + c, i), device_id_type=MESH
        )

    limits[...] = jnp.full((8, 128), 2**30, jnp.int32)
    small[0].wait()
    limits[0:1, 0:ROWS] = len_ref[...]
    lengths = limits[0:1, :]
    for u in range(2):
        first = ((z * 2 + u) * NI + i) * EXT

        def mask_tile(t, first=first, u=u):
            place = lax.broadcasted_iota(jnp.int32, (TT, 128), 0) + (first + t * TT)
            ax[u, pl.ds(pl.multiple_of(t * TT, TT), TT), :] = jnp.where(place >= lengths, MASKED, 0.0).astype(
                jnp.bfloat16
            )

        each(EXT // TT, mask_tile)
    lane = lax.broadcasted_iota(jnp.int32, (128, NQ), 1)
    row = (((lane % QD) // QB) * 2 + (lane // QD) % 2) * 4 + lane % 4
    picks = row == lax.broadcasted_iota(jnp.int32, (128, NQ), 0)
    qx[128:256, :] = jnp.where(picks, 1.0, 0.0).astype(jnp.bfloat16)
    stage[z] = q_ref[...]
    vt[128:144, :] = jnp.ones((16, TT), jnp.bfloat16)

    pl.semaphore_wait(barrier, 2 * NI - 1 + NZ - 1)

    def along_z(s):
        return remote(
            q_ref, stage.at[z], s1_send.at[s], s1_recv.at[z], (lax.rem(z + s + 1, NZ) * 2 + c, i)
        )

    each(NZ - 1, lambda s: along_z(s).start())

    @functools.partial(each, KL)
    def _(k):
        mate_kv(slot_head(k), 0).start()
        mate_kv(slot_head(k), 1).start()

    def from_z(s):
        other = lax.rem(z + s + 1, NZ)
        return remote(q_ref, stage.at[other], s1_send.at[s], s1_recv.at[other], (other * 2 + c, i))

    each(NZ - 1, lambda s: from_z(s).wait_recv())

    spread = NI // KL

    def across(s):
        k, y = s // spread, s % spread
        to = KL * y + lax.rem(j_d - k + KL, KL)
        dst = qbuf.at[j_d, half_d * 2 + c]
        sem = s2_recv.at[j_d, half_d * 2 + c]
        there = remote(stage, dst, s2_send.at[s], sem, (z * 2 + c_d, to))
        here = pltpu.make_async_copy(stage, dst, sem)
        return there, here, (to == i) & (c_d == c)

    def go(trio):
        there, here, own = trio

        @pl.when(own)
        def _():
            here.start()

        @pl.when(jnp.logical_not(own))
        def _():
            there.start()

    def gone(trio):
        there, _, own = trio

        @pl.when(jnp.logical_not(own))
        def _():
            there.wait_send()

    each(NI, lambda s: go(across(s)))

    per = EXT // TT
    blocks = NQ // CH

    def place_of(t):
        return lax.rem(c + t // per, 2), pl.ds(pl.multiple_of(lax.rem(t, per) * TT, TT), TT)

    def score(j, t, h):
        u, where = place_of(t)
        lanes = slice(h * CH, (h + 1) * CH)
        keys = jnp.concatenate([kbuf[j, u, where, :], ax[u, where, :]], axis=1)
        scores = jnp.dot(keys, qx[:, lanes], preferred_element_type=jnp.float32)
        sbuf[h % 2] = scores
        mnext[0:1, lanes] = jnp.max(scores, axis=0, keepdims=True)

    def attend(j, t):
        @pl.when(t == per - 1)
        def _():
            mate_kv(j, 0).wait_recv()
            mate_kv(j, 1).wait_recv()

        u, where = place_of(t)
        vt[0:128, :] = vbuf[j, u, where, :].T
        for h in range(blocks):
            lanes = slice(h * CH, (h + 1) * CH)
            before = mrun[0:1, lanes]
            now = jnp.maximum(before, mnext[0:1, lanes])
            if h + 1 < blocks:
                score(j, t, h + 1)
            else:
                score(j, jnp.minimum(t + 1, 2 * per - 1), 0)
            weights = jnp.exp2((sbuf[h % 2] - now) * SCALE2).astype(jnp.bfloat16)
            part = jnp.dot(vt[...], weights, preferred_element_type=jnp.float32)
            outbuf[j, :, lanes] = outbuf[j, :, lanes] * jnp.exp2((before - now) * SCALE2) + part[:136]
            mrun[0:1, lanes] = now

    def back(j, b):
        half, p = b // 2, b % 2
        to = c * half_plane + 2 * j + half
        src = outbuf.at[j, :, b * QD : (b + 1) * QD]
        there = remote(src, rbuf.at[i], r_send.at[j, b], r_recv.at[i], (z * 2 + p, to))
        here = pltpu.make_async_copy(src, rbuf.at[i], r_recv.at[i])
        return there, here, (to == i) & (c == p)

    def head_slot(k):
        j = slot_head(k)
        for b in range(4):
            pltpu.make_async_copy(stage, qbuf.at[j, b], s2_recv.at[j, b]).wait()
        qx[0:128, :] = qbuf[j].reshape(NQ, HD).T
        mrun[...] = jnp.full_like(mrun, LOWEST)
        outbuf[j] = jnp.zeros((136, NQ), jnp.float32)
        own_kv(j, 0).wait()
        own_kv(j, 1).wait()
        score(j, 0, 0)
        each(2 * per, lambda t: attend(j, t))
        outbuf[j, 129:130, :] = mrun[0:1, :]
        for b in range(4):
            go(back(j, b))

    each(KL, head_slot)

    each(
        NI,
        lambda s: pltpu.make_async_copy(rbuf.at[s], rbuf.at[s], r_recv.at[s]).wait(),
    )
    peak = lax.fori_loop(
        0, NI, lambda s, v: jnp.maximum(v, rbuf[s, 129:130, :]), jnp.full((1, QD), LOWEST, jnp.float32)
    )
    folded = lax.fori_loop(
        0,
        NI,
        lambda s, v: v + rbuf[s] * jnp.exp2((rbuf[s, 129:130, :] - peak) * SCALE2),
        jnp.zeros((136, QD), jnp.float32),
    )
    turned = folded[:128].T
    pair = jnp.concatenate(
        [jnp.broadcast_to(folded[128:129], (4, QD)), jnp.broadcast_to(peak, (4, QD))], axis=0
    )
    for d in range(NZ):
        zsend[d, 0:QB, :] = turned[d * QB : (d + 1) * QB]
        tile = (d // ZT) * LT
        zsend[d, QB : QB + 8, 0:LT] = pair[:, tile : tile + LT]

    def to_z(s):
        other = lax.rem(z + s + 1, NZ)
        return remote(zsend.at[other], zrecv.at[z], z_send.at[s], z_recv.at[z], (other * 2 + c, i))

    def of_z(s):
        other = lax.rem(z + s + 1, NZ)
        return remote(zsend.at[other], zrecv.at[other], z_send.at[s], z_recv.at[other], (other * 2 + c, i))

    each(NZ - 1, lambda s: to_z(s).start())
    zrecv[z] = zsend[z]
    each(NZ - 1, lambda s: of_z(s).wait_recv())

    for d in range(NZ):
        scal[d] = zrecv[d, QB : QB + 8, 0:LT].T
    mine = pl.ds(pl.multiple_of(lax.rem(z, ZT) * QB, QB), QB)
    sums = [scal[d, mine, 0:1] for d in range(NZ)]
    peaks = [scal[d, mine, 4:5] for d in range(NZ)]
    highest = functools.reduce(jnp.maximum, peaks)
    factors = [jnp.exp2((v - highest) * SCALE2) for v in peaks]
    total = functools.reduce(jnp.add, [f * v for f, v in zip(factors, sums)])
    result = functools.reduce(jnp.add, [f * zrecv[d, 0:QB, :] for d, f in enumerate(factors)])

    query = q_ref[...].astype(jnp.float32)
    second = lax.broadcasted_iota(jnp.int32, (QB, 1), 0) >= QB // 2
    small[1].wait()
    small[2].wait()

    def repeated(ref, e):
        four = ref[e, :, cols(i // 2)].astype(jnp.float32)
        return jnp.concatenate([four] * (QB // four.shape[0]), axis=0)

    own = [jnp.sum(query * repeated(nk_ref, e), axis=1, keepdims=True) for e in range(STEPS)]
    own[1] = jnp.where(second, own[1], LOWEST)
    top = jnp.maximum(highest, jnp.maximum(own[0], own[1]))
    factor = jnp.exp2((highest - top) * SCALE2)
    above, below = factor * result, factor * total
    for e in range(STEPS):
        w = jnp.exp2((own[e] - top) * SCALE2)
        above = above + w * repeated(nv_ref, e)
        below = below + w
    out_ref[...] = (above / below).astype(jnp.bfloat16)

    each(NZ - 1, lambda s: along_z(s).wait_send())
    each(NI, lambda s: gone(across(s)))

    def settle(j):
        mate_kv(j, 0).wait_send()
        mate_kv(j, 1).wait_send()
        for b in range(4):
            gone(back(j, b))

    each(KL, settle)
    each(NZ - 1, lambda s: to_z(s).wait_send())


def body(NO, NI, queries, key_cache, value_cache, new_keys, new_values, lengths):
    _, rows, width = queries.shape
    EXT, kv_width = key_cache.shape
    KL = kv_width // HD // 2
    heads = width // HD
    QB = STEPS * rows * heads
    NZ = NO // 2
    QD = NZ * QB
    TT = min(1024, EXT)
    CH = min(512, 2 * QD)
    LT = min(128, QD)
    q = queries.reshape(STEPS, rows, heads, HD).transpose(0, 2, 1, 3).reshape(QB, HD)
    vmem = pl.BlockSpec(memory_space=pltpu.VMEM)
    hbm = pl.BlockSpec(memory_space=pl.ANY)
    dma = pltpu.SemaphoreType.DMA
    out = pl.pallas_call(
        functools.partial(kernel, (NO, NI, KL, EXT, TT, CH, QB, lengths.shape[0])),
        out_shape=jax.ShapeDtypeStruct((QB, HD), jnp.bfloat16),
        in_specs=[vmem] + [hbm] * 5,
        out_specs=vmem,
        scratch_shapes=[
            pltpu.VMEM(new_keys.shape, jnp.bfloat16),
            pltpu.VMEM(new_values.shape, jnp.bfloat16),
            pltpu.VMEM((1, lengths.shape[0]), jnp.int32),
            pltpu.VMEM((8, 128), jnp.int32),
            pltpu.VMEM((NZ, QB, HD), jnp.bfloat16),
            pltpu.VMEM((KL, 4, NZ, QB, HD), jnp.bfloat16),
            pltpu.VMEM((KL, 2, EXT, HD), jnp.bfloat16),
            pltpu.VMEM((KL, 2, EXT, HD), jnp.bfloat16),
            pltpu.VMEM((256, 4 * QD), jnp.bfloat16),
            pltpu.VMEM((2, EXT, 128), jnp.bfloat16),
            pltpu.VMEM((8, 4 * QD), jnp.float32),
            pltpu.VMEM((8, 4 * QD), jnp.float32),
            pltpu.VMEM((2, TT, CH), jnp.float32),
            pltpu.VMEM((144, TT), jnp.bfloat16),
            pltpu.VMEM((KL, 136, 4 * QD), jnp.float32),
            pltpu.VMEM((NI, 136, QD), jnp.float32),
            pltpu.VMEM((NZ, QB + 8, HD), jnp.float32),
            pltpu.VMEM((NZ, QB + 8, HD), jnp.float32),
            pltpu.VMEM((NZ, LT, 8), jnp.float32),
            dma((3,)),
            dma((KL, 2)),
            dma((KL, 2)),
            dma((KL, 2)),
            dma((NZ,)),
            dma((NZ,)),
            dma((NI,)),
            dma((KL, 4)),
            dma((KL, 4)),
            dma((NI,)),
            dma((NZ,)),
            dma((NZ,)),
        ],
        compiler_params=pltpu.CompilerParams(
            collective_id=0, has_side_effects=True, vmem_limit_bytes=48 * 1024 * 1024
        ),
    )(q, new_keys, new_values, lengths.reshape(1, -1), key_cache, value_cache)
    return out.reshape(STEPS, heads, rows, HD).transpose(0, 2, 1, 3).reshape(queries.shape)


def solution(mesh):
    placed = (
        P(None, "outer", "inner"),
        P(("outer", "inner"), None),
        P(("outer", "inner"), None),
        P(None, "outer", None),
        P(None, "outer", None),
        P(),
    )
    return jax.shard_map(
        functools.partial(body, mesh.shape["outer"], mesh.shape["inner"]),
        mesh=mesh,
        in_specs=placed,
        out_specs=P(None, "outer", "inner"),
        check_vma=False,
    )
```
